32 devices in a mesh: gx: 16 (over z, x, core), gz: 2 (over y).
Axes of the slice: x: 2, y: 2, z: 4, core: 2. Of those that a mesh axis runs over, the one named last changes fastest.
Arguments:
- velocity: float32 [2, 2, 1, 4096, 2048], P(None, None, None, 'gx', 'gz'), may hold values from -6 to 6
- previous: float32 [2, 2, 1, 4096, 2048], P(None, None, None, 'gx', 'gz'), may hold values from -12 to 12
- base_flow: float32 [1], replicated, may hold values from -1 to 1
Outputs:
- velocity_next: float32 [2, 2, 1, 4096, 2048], P(None, None, None, 'gx', 'gz')
- nonlinear: float32 [2, 2, 1, 4096, 2048], P(None, None, None, 'gx', 'gz')
The draws below stay inside these ranges and needn't reach their ends.
All inputs are finite; a program needn't handle non-finite values.
Results may differ from the reference program's by a relative error of at most 0.00014.
Values sent between devices are 32-bit elements; how exact they have to be, the bound alone decides.
A program may use at most 128 MiB of HBM per device.

```python
import math
import jax
import jax.numpy as jnp
from jax import lax

NX = 4096
NZ = 2048
Y_WIN = 1


def block_levels(stream_key, shape, pieces, least, high):
    gain, own = 1.0, jax.random.fold_in(stream_key, 6)
    for axis_at, shards_of in pieces:
        draws = jnp.exp(jax.random.uniform(jax.random.fold_in(own, axis_at), (shards_of,), jnp.float32, least / len(pieces), high / len(pieces)))
        gain = gain * jnp.repeat(draws, shape[axis_at] // shards_of).reshape([-1 if axis == axis_at else 1 for axis in range(len(shape))])
    return gain


def normal_values(key, dims, spread, limit, split=(), kind=jnp.bfloat16):
    loudness = block_levels(key, dims, split, -0.22, 0.18) if split else 1.0
    result = jax.random.normal(key, dims, jnp.float32) * spread * loudness
    return jnp.minimum(jnp.maximum(result, -limit), limit).astype(kind)


def setup_inputs(seed: int = 0) -> dict:
    seeds = jax.random.split(jax.random.key(seed), 4)
    return {
        "velocity": normal_values(seeds[0], (2, 2, Y_WIN, NX, NZ), 1.0, 6.0, ((3, 16), (4, 2)), jnp.float32),
        "previous": normal_values(seeds[1], (2, 2, Y_WIN, NX, NZ), 2.0, 12.0, ((3, 16), (4, 2)), jnp.float32),
        "base_flow": jnp.clip(jax.random.uniform(seeds[2], (Y_WIN,), jnp.float32, -1.0, 1.0), -1.0, 1.0),
    }


VISCOSITY = 0.05
TIME_STEP = 0.2
GAMMA_NEW = 8.0 / 15.0
ZETA_OLD = -17.0 / 60.0


def signed_modes(extent):
    numbers = jnp.arange(extent, dtype=jnp.int32)
    return jnp.where(2 * numbers < extent, numbers, numbers - extent)


def one_plane(arguments):
    plane_velocity, plane_previous, plane_base = arguments
    spectra = lax.complex(plane_velocity[:, 0], plane_velocity[:, 1])
    fields = jnp.real(jnp.fft.ifft2(spectra, axes=(1, 2), norm="ortho"))
    products = jnp.stack([fields[0] * fields[0], fields[0] * fields[1], fields[1] * fields[1]])
    product_spectra = jnp.fft.fft2(products, axes=(1, 2), norm="ortho")
    prod_real = jnp.real(product_spectra)
    prod_imag = jnp.imag(product_spectra)
    modes_along = signed_modes(NX)
    modes_across = signed_modes(NZ)
    wave_along = (modes_along.astype(jnp.float32) * (2.0 * math.pi / NX))[:, None]
    wave_across = (modes_across.astype(jnp.float32) * (2.0 * math.pi / NZ))[None, :]
    keep = jnp.logical_and((3 * jnp.abs(modes_along) < NX)[:, None], (3 * jnp.abs(modes_across) < NZ)[None, :]).astype(jnp.float32)
    shear = plane_base * wave_along
    first_real = keep * (wave_along * prod_imag[0] + wave_across * prod_imag[1]) + shear * plane_velocity[0, 1]
    first_imag = -keep * (wave_along * prod_real[0] + wave_across * prod_real[1]) - shear * plane_velocity[0, 0]
    second_real = keep * (wave_along * prod_imag[1] + wave_across * prod_imag[2]) + shear * plane_velocity[1, 1]
    second_imag = -keep * (wave_along * prod_real[1] + wave_across * prod_real[2]) - shear * plane_velocity[1, 0]
    nonlinear = jnp.stack([jnp.stack([first_real, first_imag]), jnp.stack([second_real, second_imag])])
    damping = jnp.exp(-VISCOSITY * (wave_along * wave_along + wave_across * wave_across))
    advanced = damping * (plane_velocity + TIME_STEP * (GAMMA_NEW * nonlinear + ZETA_OLD * plane_previous))
    return advanced, nonlinear


def reference(velocity, previous, base_flow):
    advanced, nonlinear = lax.map(one_plane, (jnp.moveaxis(velocity, 2, 0), jnp.moveaxis(previous, 2, 0), base_flow))
    return jnp.moveaxis(advanced, 0, 2), jnp.moveaxis(nonlinear, 0, 2)
```

```python
import math

import jax
import jax.numpy as jnp
import numpy as np
from jax import lax
from jax.experimental import pallas as pl
from jax.experimental.pallas import tpu as pltpu
from jax.sharding import PartitionSpec as P

NX = 4096
NZ = 2048


TWO_PI = 2.0 * math.pi
VISCOSITY = 0.05
TIME_STEP = 0.2
GAMMA_NEW = 8.0 / 15.0
ZETA_OLD = -17.0 / 60.0


def partner_2(x, axis, distance):
    return lax.ppermute(x, axis, [(i, i ^ 1 << distance) for i in range(lax.axis_size(axis))])


def exact_einsum(pattern, left_array, right_array):
    return jnp.einsum(
        pattern,
        left_array,
        right_array,
        precision=lax.Precision.HIGHEST,
        preferred_element_type=jnp.float32,
    )


def phase_table(left_ints, right_ints, period, direction):
    phase_angle = (
        direction * TWO_PI / period * (left_ints * right_ints % period).astype(jnp.float32)
    )
    return (jnp.cos(phase_angle), jnp.sin(phase_angle))


def complex_apply(value_real, value_imag, table_real, table_imag, pattern):
    out_real = exact_einsum(pattern, value_real, table_real) - exact_einsum(
        pattern, value_imag, table_imag
    )
    out_imag = exact_einsum(pattern, value_real, table_imag) + exact_einsum(
        pattern, value_imag, table_real
    )
    return (out_real, out_imag)


def residue_of(position, levels):
    reversed_bits = jnp.zeros((), jnp.int32)
    for level in range(levels):
        reversed_bits = reversed_bits + ((position >> level & 1) << levels - 1 - level)
    return reversed_bits


def section_twiddle(position, half_span):
    phase_angle = TWO_PI / (2 * half_span) * (position % half_span).astype(jnp.float32)
    return (jnp.cos(phase_angle), jnp.sin(phase_angle))


def spread_butterfly(values):
    position = lax.axis_index("gx")
    levels = lax.axis_size("gx").bit_length() - 1
    for level in reversed(range(levels)):
        half_span = 1 << level
        partner = partner_2(values, "gx", level)
        upper_half = position >> level & 1 == 1
        cosine, sine_part = section_twiddle(position, half_span)
        difference = partner - values
        rotated = jnp.stack(
            [
                difference[:, 0] * cosine - difference[:, 1] * sine_part,
                difference[:, 0] * sine_part + difference[:, 1] * cosine,
            ],
            axis=1,
        )
        values = jnp.where(upper_half, rotated, values + partner)
    return (values, residue_of(position, levels))


def gather_butterfly(values):
    position = lax.axis_index("gx")
    levels = lax.axis_size("gx").bit_length() - 1
    for level in range(levels):
        half_span = 1 << level
        partner = partner_2(values, "gx", level)
        upper_half = position >> level & 1 == 1
        cosine, sine_part = section_twiddle(position, half_span)
        upper_item = jnp.where(upper_half, values, partner)
        lower_item = jnp.where(upper_half, partner, values)
        turned = jnp.stack(
            [
                upper_item[:, 0] * cosine + upper_item[:, 1] * sine_part,
                upper_item[:, 1] * cosine - upper_item[:, 0] * sine_part,
            ],
            axis=1,
        )
        values = jnp.where(upper_half, lower_item - turned, lower_item + turned)
    return values


def axial_table(residue, mode_count, device_count):
    numbers = jnp.arange(mode_count, dtype=jnp.int32)
    points = residue + device_count * numbers
    cosine, sine_part = phase_table(points[:, None], numbers[None, :], NX, 1.0)
    norm_scale = 1.0 / math.sqrt(NX)
    return (cosine * norm_scale, sine_part * norm_scale)


def span_table(groups, span_size):
    residues = jnp.arange(groups, dtype=jnp.int32)[:, None, None]
    grid_rows = jnp.arange(span_size, dtype=jnp.int32)[None, :, None]
    mode_cols = jnp.arange(span_size, dtype=jnp.int32)[None, None, :]
    cosine, sine_part = phase_table(mode_cols, residues + groups * grid_rows, NZ, 1.0)
    norm_scale = 1.0 / math.sqrt(NZ)
    return (cosine * norm_scale, sine_part * norm_scale)


def spanwise_work(received):
    fields, pair_size, planes, row_count, extent = received.shape
    groups = lax.axis_size("gz")
    span_size = extent // groups
    blocks = received.reshape(fields, pair_size, planes, row_count, groups, span_size)
    group_ids = jnp.arange(groups, dtype=jnp.int32)
    mix_real, mix_imag = phase_table(group_ids[:, None], group_ids[None, :], groups, 1.0)
    section_real, section_imag = complex_apply(
        blocks[:, 0], blocks[:, 1], mix_real, mix_imag, "fylcj,rc->fylrj"
    )
    table_real, table_imag = span_table(groups, span_size)
    physical = exact_einsum("fylrj,rtj->fylrt", section_real, table_real) - exact_einsum(
        "fylrj,rtj->fylrt", section_imag, table_imag
    )
    products = jnp.stack(
        [physical[0] * physical[0], physical[0] * physical[1], physical[1] * physical[1]]
    )
    back_real = exact_einsum("pylrt,rtj->pylrj", products, table_real)
    back_imag = -exact_einsum("pylrt,rtj->pylrj", products, table_imag)
    out_real, out_imag = complex_apply(back_real, back_imag, mix_real, -mix_imag, "pylrj,cr->pylcj")
    spectra = jnp.stack([out_real, out_imag], axis=1)
    return spectra.reshape(3, pair_size, planes, row_count, extent)


def span_round(values, work):
    span_spectra = work(lax.all_to_all(values, "gz", split_axis=3, concat_axis=4, tiled=True))
    return lax.all_to_all(span_spectra, "gz", split_axis=4, concat_axis=3, tiled=True)


def signed_block(start, mode_count, extent):
    numbers = start + jnp.arange(mode_count, dtype=jnp.int32)
    return jnp.where(2 * numbers < extent, numbers, numbers - extent)


def local(velocity, previous, base_flow):
    mode_count = velocity.shape[3]
    span_size = velocity.shape[4]
    device_count = lax.axis_size("gx")
    spread, residue = spread_butterfly(velocity)
    table_real, table_imag = axial_table(residue, mode_count, device_count)
    along_real, along_imag = complex_apply(
        spread[:, 0], spread[:, 1], table_real, table_imag, "fymq,sm->fysq"
    )
    physical_along = jnp.stack([along_real, along_imag], axis=1)
    returned = span_round(physical_along, spanwise_work)
    local_real, local_imag = complex_apply(
        returned[:, 0], returned[:, 1], table_real.T, -table_imag.T, "fysq,ms->fymq"
    )
    local_spectra = jnp.stack([local_real, local_imag], axis=1)
    product_spectra = gather_butterfly(local_spectra)
    modes_along = signed_block(lax.axis_index("gx") * mode_count, mode_count, NX)
    modes_across = signed_block(lax.axis_index("gz") * span_size, span_size, NZ)
    wave_along = (modes_along.astype(jnp.float32) * (TWO_PI / NX))[:, None]
    wave_across = (modes_across.astype(jnp.float32) * (TWO_PI / NZ))[None, :]
    keep = jnp.logical_and(
        (3 * jnp.abs(modes_along) < NX)[:, None], (3 * jnp.abs(modes_across) < NZ)[None, :]
    ).astype(jnp.float32)
    shear = base_flow[:, None, None] * wave_along[None]
    prod_real = product_spectra[:, 0]
    prod_imag = product_spectra[:, 1]
    first_real = (
        keep * (wave_along * prod_imag[0] + wave_across * prod_imag[1]) + shear * velocity[0, 1]
    )
    first_imag = (
        -keep * (wave_along * prod_real[0] + wave_across * prod_real[1]) - shear * velocity[0, 0]
    )
    second_real = (
        keep * (wave_along * prod_imag[1] + wave_across * prod_imag[2]) + shear * velocity[1, 1]
    )
    second_imag = (
        -keep * (wave_along * prod_real[1] + wave_across * prod_real[2]) - shear * velocity[1, 0]
    )
    nonlinear = jnp.stack(
        [jnp.stack([first_real, first_imag]), jnp.stack([second_real, second_imag])]
    )
    damping = jnp.exp(-VISCOSITY * (wave_along * wave_along + wave_across * wave_across))
    advanced = damping * (velocity + TIME_STEP * (GAMMA_NEW * nonlinear + ZETA_OLD * previous))
    return (advanced, nonlinear)


XR = 16
XS = NX // XR
ZR = 8
ZS = NZ // ZR
LOW = (0, 1, 2)
HIGH = (5, 6, 7)
MIB = 1 << 20


def split_table(table):
    high = table.astype(np.float32).astype(jnp.bfloat16)
    low = (table - high.astype(np.float64)).astype(np.float32).astype(jnp.bfloat16)
    return high, low


def z_table():
    r = np.arange(ZR)[:, None, None]
    b = np.arange(ZS)[None, :, None]
    s = np.arange(ZS)[None, None, :]
    angle = TWO_PI / NZ * ((b * (r + ZR * s)) % NZ)
    cos, sin = np.cos(angle) / math.sqrt(NZ), np.sin(angle) / math.sqrt(NZ)
    top = np.concatenate([cos, sin], axis=2)
    bottom = np.concatenate([-sin, cos], axis=2)
    return split_table(np.concatenate([top, bottom], axis=1))


def x_table():
    r = np.arange(XR)[:, None, None]
    s = np.arange(XS)[None, :, None]
    m = np.arange(XS)[None, None, :]
    angle = TWO_PI / NX * ((m * (r + XR * s)) % NX)
    cos, sin = np.cos(angle) / math.sqrt(NX), np.sin(angle) / math.sqrt(NX)
    return split_table(np.concatenate([cos, -sin], axis=2))


def turn(value, numerator, size, sign):
    re, im = value
    numerator = numerator % size
    if numerator == 0:
        return re, im
    if 4 * numerator == size:
        return (-im, re) if sign > 0 else (im, -re)
    if 8 * numerator == size:
        h = math.sqrt(0.5)
        return ((re - im) * h, (re + im) * h) if sign > 0 else ((re + im) * h, (im - re) * h)
    if 8 * numerator == 3 * size:
        h = math.sqrt(0.5)
        return ((-re - im) * h, (re - im) * h) if sign > 0 else ((im - re) * h, (-re - im) * h)
    c = math.cos(TWO_PI * numerator / size)
    s = sign * math.sin(TWO_PI * numerator / size)
    return re * c - im * s, re * s + im * c


def small_dft(values, sign):
    size = len(values)
    if size == 1:
        return values
    even = small_dft(values[0::2], sign)
    odd = small_dft(values[1::2], sign)
    half = size // 2
    out = [None] * size
    for i in range(half):
        re, im = turn(odd[i], i, size, sign)
        out[i] = (even[i][0] + re, even[i][1] + im)
        out[i + half] = (even[i][0] - re, even[i][1] - im)
    return out


def parts_of(value):
    high = value.astype(jnp.bfloat16)
    return high, (value - high.astype(jnp.float32)).astype(jnp.bfloat16)


def dot3(a_high, a_low, b_high, b_low, dims):
    def dot(a, b):
        return lax.dot_general(a, b, (dims, ((), ())), preferred_element_type=jnp.float32)

    return dot(a_high, b_high) + (dot(a_high, b_low) + dot(a_low, b_high))


def merge(first, second, low_half):
    return (
        jnp.where(low_half, first, pltpu.roll(second, 64, 1)),
        jnp.where(low_half, pltpu.roll(first, 64, 1), second),
    )


def z_inverse_kernel(v_ref, high_ref, low_ref, out_ref, th_ref, tl_ref):
    rows = v_ref.shape[3]
    step = 16
    for c in range(2):
        def body(i, carry):
            at = pl.multiple_of(i * step, step)
            for lane in range(0, ZS, 128):
                values = [
                    tuple(
                        v_ref[c, p, a // 4, pl.ds(at, step), pl.ds((a % 4) * ZS + lane, 128)]
                        for p in range(2)
                    )
                    for a in range(ZR)
                ]
                for r, pair in enumerate(small_dft(values, 1)):
                    for p in range(2):
                        high, low = parts_of(pair[p])
                        th_ref[r, pl.ds(c * rows + at, step), pl.ds(p * ZS + lane, 128)] = high
                        tl_ref[r, pl.ds(c * rows + at, step), pl.ds(p * ZS + lane, 128)] = low
            return carry
        lax.fori_loop(0, rows // step, body, 0)

    def group(r, carry):
        done = dot3(th_ref[r], tl_ref[r], high_ref[r], low_ref[r], ((1,), (0,)))
        low_half = lax.broadcasted_iota(jnp.int32, (rows, 128), 1) < 64
        for p in range(2):
            for t in range(2):
                at = p * ZS + t * 128
                even, odd = merge(done[:rows, at : at + 128], done[rows:, at : at + 128], low_half)
                out_ref[r, 2 * t, p] = even
                out_ref[r, 2 * t + 1, p] = odd
        return carry
    lax.fori_loop(0, ZR, group, 0)


def x_kernel(v_ref, ih_ref, il_ref, fh_ref, fl_ref, out_ref, th_ref, tl_ref, u_ref):
    rows = v_ref.shape[3]
    step = 16
    for r in range(2):
        def body(i, carry):
            at = pl.multiple_of(i * step, step)
            values = [
                tuple(v_ref[g, r, p, pl.ds(at, step), :] for p in range(2)) for g in range(XR)
            ]
            for res, pair in enumerate(small_dft(values, 1)):
                for p in range(2):
                    high, low = parts_of(pair[p])
                    th_ref[res, pl.ds(p * XS + r * rows + at, step), :] = high
                    tl_ref[res, pl.ds(p * XS + r * rows + at, step), :] = low
            return carry
        lax.fori_loop(0, rows // step, body, 0)

    def residue(res, carry):
        field = dot3(ih_ref[res], il_ref[res], th_ref[res], tl_ref[res], ((1,), (0,)))
        swapped = pltpu.roll(field, 64, 1)
        products = jnp.concatenate([field * field, field * swapped], axis=1)
        high, low = parts_of(products)
        u_ref[res] = dot3(fh_ref[res], fl_ref[res], high, low, ((1,), (0,)))
        return carry
    lax.fori_loop(0, XR, residue, 0)

    low_half = lax.broadcasted_iota(jnp.int32, (8, 128), 1) < 64
    for r in range(2):
        def back(i, carry):
            at = pl.multiple_of(i * 8, 8)
            for h in range(2):
                values = [
                    tuple(
                        u_ref[res, pl.ds(p * XS + r * rows + at, 8), pl.ds(h * 128, 128)]
                        for p in range(2)
                    )
                    for res in range(XR)
                ]
                for g, (re, im) in enumerate(small_dft(values, -1)):
                    if h == 0:
                        out_ref[g, r, 0, pl.ds(at, 8), :] = re
                        out_ref[g, r, 1, pl.ds(at, 8), :] = im
                    else:
                        out_ref[g, r, 2, pl.ds(at, 8), :] = jnp.where(low_half, re, im)
            return carry
        lax.fori_loop(0, rows // 8, back, 0)


def z_forward_kernel(v_ref, high_ref, low_ref, wave_ref, keep_ref, out_ref, w_ref):
    rows = v_ref.shape[3]
    low_half = lax.broadcasted_iota(jnp.int32, (rows, 128), 1) < 64

    def group(r, carry):
        real, imag, mixed = ([v_ref[r, j, x] for j in range(4)] for x in range(3))
        p0r, p2r, p0i, p2i, p1r, p1i = [], [], [], [], [], []
        for source, first, second in ((real, p0r, p2r), (imag, p0i, p2i), (mixed, p1r, p1i)):
            for t in range(2):
                a, b = merge(source[2 * t], source[2 * t + 1], low_half)
                first.append(a)
                second.append(b)
        lines = jnp.concatenate(
            [jnp.concatenate(x, axis=1) for x in (p0r + p0i, p1r + p1i, p2r + p2i)], axis=0
        )
        high, low = parts_of(lines)
        w_ref[r] = dot3(high, low, high_ref[r], low_ref[r], ((1,), (1,)))
        return carry
    lax.fori_loop(0, ZR, group, 0)

    def body(i, carry):
        at = pl.multiple_of(i * 8, 8)
        wave_along = wave_ref[pl.ds(at, 8), :]
        keep_along = keep_ref[pl.ds(at, 8), :]
        for lane in range(0, ZS, 128):
            spectra = []
            for j in range(3):
                values = [
                    tuple(
                        w_ref[r, pl.ds(j * rows + at, 8), pl.ds(p * ZS + lane, 128)]
                        for p in range(2)
                    )
                    for r in range(ZR)
                ]
                spectra.append(small_dft(values, -1))
            for half, groups in enumerate((LOW, HIGH)):
                for place, a in enumerate(groups):
                    start = a * ZS + lane - (NZ if half else 0)
                    mode = start + lax.broadcasted_iota(jnp.int32, (8, 128), 1)
                    wave_across = mode.astype(jnp.float32) * (TWO_PI / NZ)
                    keep = jnp.where(3 * jnp.abs(mode) < NZ, keep_along, 0.0)
                    (ar, ai), (br, bi), (cr, ci) = (x[a] for x in spectra)
                    to = (pl.ds(at, 8), pl.ds(place * ZS + lane, 128))
                    out_ref[(half, 0) + to] = keep * (wave_along * ai + wave_across * bi)
                    out_ref[(half, 1) + to] = -keep * (wave_along * ar + wave_across * br)
                    out_ref[(half, 2) + to] = keep * (wave_along * bi + wave_across * ci)
                    out_ref[(half, 3) + to] = -keep * (wave_along * br + wave_across * cr)
        return carry
    lax.fori_loop(0, rows // 8, body, 0)


def advance_kernel(half_ref, base_ref, v_ref, old_ref, term_ref, along_ref, across_ref, next_ref, non_ref):
    rows, extent = v_ref.shape[2:]
    wave_along = along_ref[:, :1]
    wave_across = across_ref[:1, :]
    damping = jnp.exp(-VISCOSITY * (wave_along * wave_along + wave_across * wave_across))
    shear = base_ref[0] * wave_along
    empty = jnp.zeros((rows, extent - term_ref.shape[3]), jnp.float32)
    for c in range(2):
        for p in range(2):
            term = term_ref[0, 2 * c + p]
            term = jnp.where(
                half_ref[0] == 0,
                jnp.concatenate([term, empty], axis=1),
                jnp.concatenate([empty, term], axis=1),
            )
            other = shear * v_ref[c, 1 - p]
            result = term + other if p == 0 else term - other
            non_ref[c, p] = result
            next_ref[c, p] = damping * (
                v_ref[c, p] + TIME_STEP * (GAMMA_NEW * result + ZETA_OLD * old_ref[c, p])
            )


def whole(*_):
    return pl.BlockSpec(memory_space=pltpu.VMEM)


def params(limit):
    return pltpu.CompilerParams(vmem_limit_bytes=limit * MIB)


def lines_local(velocity, previous, base_flow):
    velocity, previous = velocity[:, :, 0], previous[:, :, 0]
    mode_count, extent = velocity.shape[2:]
    rows = mode_count // 2
    gx, gz = lax.axis_index("gx"), lax.axis_index("gz")
    f32, bf16 = jnp.float32, jnp.bfloat16
    zh, zl = z_table()
    xh, xl = x_table()
    fh, fl = np.swapaxes(xh, 1, 2), np.swapaxes(xl, 1, 2)

    lines = lax.all_to_all(
        velocity.reshape(2, 2, 2, rows, extent), "gz", split_axis=2, concat_axis=2, tiled=True
    )
    along_z = pl.pallas_call(
        z_inverse_kernel,
        out_shape=jax.ShapeDtypeStruct((ZR, 4, 2, rows, 128), f32),
        in_specs=[whole()] * 3,
        out_specs=whole(),
        scratch_shapes=[pltpu.VMEM((ZR, 2 * rows, 2 * ZS), bf16)] * 2,
        compiler_params=params(48),
        name="z_inverse",
    )(lines, zh, zl)
    swapped = exchange(along_z.reshape(32, 2, rows, 128))
    worked = pl.pallas_call(
        x_kernel,
        out_shape=jax.ShapeDtypeStruct((XR, 2, 3, rows, 128), f32),
        in_specs=[whole()] * 5,
        out_specs=whole(),
        scratch_shapes=[pltpu.VMEM((XR, 2 * XS, 128), bf16)] * 2
        + [pltpu.VMEM((XR, 2 * XS, 256), f32)],
        compiler_params=params(56),
        name="x_work",
    )(swapped.reshape(XR, 2, 2, rows, 128), xh, xl, fh, fl)
    returned = exchange(worked.reshape(32, 3, rows, 128))

    def modes(start, count, size):
        numbers = start + jnp.arange(count, dtype=jnp.int32)
        return jnp.where(2 * numbers < size, numbers, numbers - size)

    own = modes(gx * mode_count + gz * rows, rows, NX)[:, None]
    own_wave = jnp.broadcast_to(own.astype(f32) * (TWO_PI / NX), (rows, 128))
    own_keep = jnp.broadcast_to((3 * jnp.abs(own) < NX).astype(f32), (rows, 128))
    active = len(LOW) * ZS
    terms = pl.pallas_call(
        z_forward_kernel,
        out_shape=jax.ShapeDtypeStruct((2, 4, rows, active), f32),
        in_specs=[whole()] * 5,
        out_specs=whole(),
        scratch_shapes=[pltpu.VMEM((ZR, 3 * rows, 2 * ZS), f32)],
        compiler_params=params(48),
        name="z_forward",
    )(returned.reshape(ZR, 4, 3, rows, 128), zh, zl, own_wave, own_keep)
    terms = lax.all_to_all(terms, "gz", split_axis=0, concat_axis=0, tiled=True)

    along = modes(gx * mode_count, mode_count, NX).astype(f32) * (TWO_PI / NX)
    across = modes(gz * extent, extent, NZ).astype(f32) * (TWO_PI / NZ)
    block = 64
    per = rows // block
    scalar = pl.BlockSpec(memory_space=pltpu.SMEM)
    field = pl.BlockSpec((2, 2, block, extent), lambda i: (0, 0, i, 0))
    advanced, nonlinear = pl.pallas_call(
        advance_kernel,
        grid=(mode_count // block,),
        out_shape=[jax.ShapeDtypeStruct(velocity.shape, f32)] * 2,
        in_specs=[
            scalar,
            scalar,
            field,
            field,
            pl.BlockSpec((1, 4, block, active), lambda i: (i // per, 0, i % per, 0)),
            pl.BlockSpec((block, 128), lambda i: (i, 0)),
            pl.BlockSpec((8, extent), lambda i: (0, 0)),
        ],
        out_specs=[field, field],
        compiler_params=params(48),
        name="advance",
    )(
        gz.astype(jnp.int32)[None],
        base_flow,
        velocity,
        previous,
        terms,
        jnp.broadcast_to(along[:, None], (mode_count, 128)),
        jnp.broadcast_to(across[None], (8, extent)),
    )
    return advanced[:, :, None], nonlinear[:, :, None]


def exchange(value):
    return lax.all_to_all(value, ("gx", "gz"), split_axis=0, concat_axis=0, tiled=True)


def solution(mesh):
    in_specs = (P(None, None, None, "gx", "gz"), P(None, None, None, "gx", "gz"), P())
    out_specs = (P(None, None, None, "gx", "gz"), P(None, None, None, "gx", "gz"))
    fits = mesh.shape["gx"] == XR and mesh.shape["gz"] == 2
    work = lines_local if fits else local
    return jax.shard_map(work, mesh=mesh, in_specs=in_specs, out_specs=out_specs, check_vma=False)
```

```python
import functools
import math

import jax
import jax.numpy as jnp
import numpy as np
from jax import lax
from jax.experimental import pallas as pl
from jax.experimental.pallas import tpu as pltpu
from jax.sharding import PartitionSpec as P

NX = 4096
NZ = 2048


TWO_PI = 2.0 * math.pi
VISCOSITY = 0.05
TIME_STEP = 0.2
GAMMA_NEW = 8.0 / 15.0
ZETA_OLD = -17.0 / 60.0


def partner_2(x, axis, distance):
    return lax.ppermute(x, axis, [(i, i ^ 1 << distance) for i in range(lax.axis_size(axis))])


def exact_einsum(pattern, left_array, right_array):
    return jnp.einsum(
        pattern,
        left_array,
        right_array,
        precision=lax.Precision.HIGHEST,
        preferred_element_type=jnp.float32,
    )


def phase_table(left_ints, right_ints, period, direction):
    phase_angle = (
        direction * TWO_PI / period * (left_ints * right_ints % period).astype(jnp.float32)
    )
    return (jnp.cos(phase_angle), jnp.sin(phase_angle))


def complex_apply(value_real, value_imag, table_real, table_imag, pattern):
    out_real = exact_einsum(pattern, value_real, table_real) - exact_einsum(
        pattern, value_imag, table_imag
    )
    out_imag = exact_einsum(pattern, value_real, table_imag) + exact_einsum(
        pattern, value_imag, table_real
    )
    return (out_real, out_imag)


def residue_of(position, levels):
    reversed_bits = jnp.zeros((), jnp.int32)
    for level in range(levels):
        reversed_bits = reversed_bits + ((position >> level & 1) << levels - 1 - level)
    return reversed_bits


def section_twiddle(position, half_span):
    phase_angle = TWO_PI / (2 * half_span) * (position % half_span).astype(jnp.float32)
    return (jnp.cos(phase_angle), jnp.sin(phase_angle))


def spread_butterfly(values):
    position = lax.axis_index("gx")
    levels = lax.axis_size("gx").bit_length() - 1
    for level in reversed(range(levels)):
        half_span = 1 << level
        partner = partner_2(values, "gx", level)
        upper_half = position >> level & 1 == 1
        cosine, sine_part = section_twiddle(position, half_span)
        difference = partner - values
        rotated = jnp.stack(
            [
                difference[:, 0] * cosine - difference[:, 1] * sine_part,
                difference[:, 0] * sine_part + difference[:, 1] * cosine,
            ],
            axis=1,
        )
        values = jnp.where(upper_half, rotated, values + partner)
    return (values, residue_of(position, levels))


def gather_butterfly(values):
    position = lax.axis_index("gx")
    levels = lax.axis_size("gx").bit_length() - 1
    for level in range(levels):
        half_span = 1 << level
        partner = partner_2(values, "gx", level)
        upper_half = position >> level & 1 == 1
        cosine, sine_part = section_twiddle(position, half_span)
        upper_item = jnp.where(upper_half, values, partner)
        lower_item = jnp.where(upper_half, partner, values)
        turned = jnp.stack(
            [
                upper_item[:, 0] * cosine + upper_item[:, 1] * sine_part,
                upper_item[:, 1] * cosine - upper_item[:, 0] * sine_part,
            ],
            axis=1,
        )
        values = jnp.where(upper_half, lower_item - turned, lower_item + turned)
    return values


def axial_table(residue, mode_count, device_count):
    numbers = jnp.arange(mode_count, dtype=jnp.int32)
    points = residue + device_count * numbers
    cosine, sine_part = phase_table(points[:, None], numbers[None, :], NX, 1.0)
    norm_scale = 1.0 / math.sqrt(NX)
    return (cosine * norm_scale, sine_part * norm_scale)


def span_table(groups, span_size):
    residues = jnp.arange(groups, dtype=jnp.int32)[:, None, None]
    grid_rows = jnp.arange(span_size, dtype=jnp.int32)[None, :, None]
    mode_cols = jnp.arange(span_size, dtype=jnp.int32)[None, None, :]
    cosine, sine_part = phase_table(mode_cols, residues + groups * grid_rows, NZ, 1.0)
    norm_scale = 1.0 / math.sqrt(NZ)
    return (cosine * norm_scale, sine_part * norm_scale)


def spanwise_work(received):
    fields, pair_size, planes, row_count, extent = received.shape
    groups = lax.axis_size("gz")
    span_size = extent // groups
    blocks = received.reshape(fields, pair_size, planes, row_count, groups, span_size)
    group_ids = jnp.arange(groups, dtype=jnp.int32)
    mix_real, mix_imag = phase_table(group_ids[:, None], group_ids[None, :], groups, 1.0)
    section_real, section_imag = complex_apply(
        blocks[:, 0], blocks[:, 1], mix_real, mix_imag, "fylcj,rc->fylrj"
    )
    table_real, table_imag = span_table(groups, span_size)
    physical = exact_einsum("fylrj,rtj->fylrt", section_real, table_real) - exact_einsum(
        "fylrj,rtj->fylrt", section_imag, table_imag
    )
    products = jnp.stack(
        [physical[0] * physical[0], physical[0] * physical[1], physical[1] * physical[1]]
    )
    back_real = exact_einsum("pylrt,rtj->pylrj", products, table_real)
    back_imag = -exact_einsum("pylrt,rtj->pylrj", products, table_imag)
    out_real, out_imag = complex_apply(back_real, back_imag, mix_real, -mix_imag, "pylrj,cr->pylcj")
    spectra = jnp.stack([out_real, out_imag], axis=1)
    return spectra.reshape(3, pair_size, planes, row_count, extent)


def span_round(values, work):
    span_spectra = work(lax.all_to_all(values, "gz", split_axis=3, concat_axis=4, tiled=True))
    return lax.all_to_all(span_spectra, "gz", split_axis=4, concat_axis=3, tiled=True)


def signed_block(start, mode_count, extent):
    numbers = start + jnp.arange(mode_count, dtype=jnp.int32)
    return jnp.where(2 * numbers < extent, numbers, numbers - extent)


def local(velocity, previous, base_flow):
    mode_count = velocity.shape[3]
    span_size = velocity.shape[4]
    device_count = lax.axis_size("gx")
    spread, residue = spread_butterfly(velocity)
    table_real, table_imag = axial_table(residue, mode_count, device_count)
    along_real, along_imag = complex_apply(
        spread[:, 0], spread[:, 1], table_real, table_imag, "fymq,sm->fysq"
    )
    physical_along = jnp.stack([along_real, along_imag], axis=1)
    returned = span_round(physical_along, spanwise_work)
    local_real, local_imag = complex_apply(
        returned[:, 0], returned[:, 1], table_real.T, -table_imag.T, "fysq,ms->fymq"
    )
    local_spectra = jnp.stack([local_real, local_imag], axis=1)
    product_spectra = gather_butterfly(local_spectra)
    modes_along = signed_block(lax.axis_index("gx") * mode_count, mode_count, NX)
    modes_across = signed_block(lax.axis_index("gz") * span_size, span_size, NZ)
    wave_along = (modes_along.astype(jnp.float32) * (TWO_PI / NX))[:, None]
    wave_across = (modes_across.astype(jnp.float32) * (TWO_PI / NZ))[None, :]
    keep = jnp.logical_and(
        (3 * jnp.abs(modes_along) < NX)[:, None], (3 * jnp.abs(modes_across) < NZ)[None, :]
    ).astype(jnp.float32)
    shear = base_flow[:, None, None] * wave_along[None]
    prod_real = product_spectra[:, 0]
    prod_imag = product_spectra[:, 1]
    first_real = (
        keep * (wave_along * prod_imag[0] + wave_across * prod_imag[1]) + shear * velocity[0, 1]
    )
    first_imag = (
        -keep * (wave_along * prod_real[0] + wave_across * prod_real[1]) - shear * velocity[0, 0]
    )
    second_real = (
        keep * (wave_along * prod_imag[1] + wave_across * prod_imag[2]) + shear * velocity[1, 1]
    )
    second_imag = (
        -keep * (wave_along * prod_real[1] + wave_across * prod_real[2]) - shear * velocity[1, 0]
    )
    nonlinear = jnp.stack(
        [jnp.stack([first_real, first_imag]), jnp.stack([second_real, second_imag])]
    )
    damping = jnp.exp(-VISCOSITY * (wave_along * wave_along + wave_across * wave_across))
    advanced = damping * (velocity + TIME_STEP * (GAMMA_NEW * nonlinear + ZETA_OLD * previous))
    return (advanced, nonlinear)


XR = 16
XS = NX // XR
ZR = 8
ZS = NZ // ZR
LOW = (0, 1, 2)
HIGH = (5, 6, 7)
MIB = 1 << 20
PIECES = 2


def split_table(table):
    high = table.astype(np.float32).astype(jnp.bfloat16)
    low = (table - high.astype(np.float64)).astype(np.float32).astype(jnp.bfloat16)
    return high, low


def z_table():
    r = np.arange(ZR)[:, None, None]
    b = np.arange(ZS)[None, :, None]
    s = np.arange(ZS)[None, None, :]
    angle = TWO_PI / NZ * ((b * (r + ZR * s)) % NZ)
    cos, sin = np.cos(angle) / math.sqrt(NZ), np.sin(angle) / math.sqrt(NZ)
    top = np.concatenate([cos, sin], axis=2)
    bottom = np.concatenate([-sin, cos], axis=2)
    return split_table(np.concatenate([top, bottom], axis=1))


def x_table():
    r = np.arange(XR)[:, None, None]
    s = np.arange(XS)[None, :, None]
    m = np.arange(XS)[None, None, :]
    angle = TWO_PI / NX * ((m * (r + XR * s)) % NX)
    cos, sin = np.cos(angle) / math.sqrt(NX), np.sin(angle) / math.sqrt(NX)
    return split_table(np.concatenate([cos, -sin], axis=2))


def turn(value, numerator, size, sign):
    re, im = value
    numerator = numerator % size
    if numerator == 0:
        return re, im
    if 4 * numerator == size:
        return (-im, re) if sign > 0 else (im, -re)
    if 8 * numerator == size:
        h = math.sqrt(0.5)
        return ((re - im) * h, (re + im) * h) if sign > 0 else ((re + im) * h, (im - re) * h)
    if 8 * numerator == 3 * size:
        h = math.sqrt(0.5)
        return ((-re - im) * h, (re - im) * h) if sign > 0 else ((im - re) * h, (-re - im) * h)
    c = math.cos(TWO_PI * numerator / size)
    s = sign * math.sin(TWO_PI * numerator / size)
    return re * c - im * s, re * s + im * c


def small_dft(values, sign):
    size = len(values)
    if size == 1:
        return values
    even = small_dft(values[0::2], sign)
    odd = small_dft(values[1::2], sign)
    half = size // 2
    out = [None] * size
    for i in range(half):
        re, im = turn(odd[i], i, size, sign)
        out[i] = (even[i][0] + re, even[i][1] + im)
        out[i + half] = (even[i][0] - re, even[i][1] - im)
    return out


def parts_of(value):
    high = value.astype(jnp.bfloat16)
    return high, (value - high.astype(jnp.float32)).astype(jnp.bfloat16)


def dot3(a_high, a_low, b_high, b_low, dims):
    def dot(a, b):
        return lax.dot_general(a, b, (dims, ((), ())), preferred_element_type=jnp.float32)

    return dot(a_high, b_high) + (dot(a_high, b_low) + dot(a_low, b_high))


def merge(first, second, low_half):
    return (
        jnp.where(low_half, first, pltpu.roll(second, 64, 1)),
        jnp.where(low_half, pltpu.roll(first, 64, 1), second),
    )


def z_inverse_kernel(half_ref, own_ref, other_ref, high_ref, low_ref, out_ref, th_ref, tl_ref):
    rows = own_ref.shape[2]
    step = 16
    first = half_ref[0] == 0
    for c in range(2):
        def body(i, carry):
            at = pl.multiple_of(i * step, step)
            for lane in range(0, ZS, 128):
                values = [None] * ZR
                for a in range(ZR // 2):
                    to = (pl.ds(at, step), pl.ds(a * ZS + lane, 128))
                    own = [own_ref[(c, p) + to] for p in range(2)]
                    other = [other_ref[(c, p) + to] for p in range(2)]
                    values[a] = tuple(jnp.where(first, x, y) for x, y in zip(own, other))
                    values[a + ZR // 2] = tuple(jnp.where(first, y, x) for x, y in zip(own, other))
                for r, pair in enumerate(small_dft(values, 1)):
                    for p in range(2):
                        high, low = parts_of(pair[p])
                        th_ref[r, pl.ds(c * rows + at, step), pl.ds(p * ZS + lane, 128)] = high
                        tl_ref[r, pl.ds(c * rows + at, step), pl.ds(p * ZS + lane, 128)] = low
            return carry
        lax.fori_loop(0, rows // step, body, 0)

    def group(r, carry):
        done = dot3(th_ref[r], tl_ref[r], high_ref[r], low_ref[r], ((1,), (0,)))
        low_half = lax.broadcasted_iota(jnp.int32, (rows, 128), 1) < 64
        for p in range(2):
            for t in range(2):
                at = p * ZS + t * 128
                even, odd = merge(done[:rows, at : at + 128], done[rows:, at : at + 128], low_half)
                out_ref[r, 2 * t, p] = even
                out_ref[r, 2 * t + 1, p] = odd
        return carry
    lax.fori_loop(0, ZR, group, 0)


def x_kernel(*refs):
    v_refs, (ih_ref, il_ref, fh_ref, fl_ref) = refs[:PIECES], refs[PIECES : PIECES + 4]
    out_refs = refs[PIECES + 4 : 2 * PIECES + 4]
    th_ref, tl_ref, u_ref = refs[2 * PIECES + 4 :]
    rows = v_refs[0].shape[3]
    step = 16
    for r, h in ((r, h) for r in range(2) for h in range(PIECES)):
        v_ref, base = v_refs[h], (r * PIECES + h) * rows

        def body(i, carry):
            at = pl.multiple_of(i * step, step)
            values = [
                tuple(v_ref[g, r, p, pl.ds(at, step), :] for p in range(2)) for g in range(XR)
            ]
            for res, pair in enumerate(small_dft(values, 1)):
                for p in range(2):
                    high, low = parts_of(pair[p])
                    th_ref[res, pl.ds(p * XS + base + at, step), :] = high
                    tl_ref[res, pl.ds(p * XS + base + at, step), :] = low
            return carry
        lax.fori_loop(0, rows // step, body, 0)

    def residue(res, carry):
        field = dot3(ih_ref[res], il_ref[res], th_ref[res], tl_ref[res], ((1,), (0,)))
        swapped = pltpu.roll(field, 64, 1)
        products = jnp.concatenate([field * field, field * swapped], axis=1)
        high, low = parts_of(products)
        u_ref[res] = dot3(fh_ref[res], fl_ref[res], high, low, ((1,), (0,)))
        return carry
    lax.fori_loop(0, XR, residue, 0)

    low_half = lax.broadcasted_iota(jnp.int32, (8, 128), 1) < 64
    for r, n in ((r, n) for r in range(2) for n in range(PIECES)):
        out_ref, base = out_refs[n], (r * PIECES + n) * rows

        def back(i, carry):
            at = pl.multiple_of(i * 8, 8)
            for h in range(2):
                values = [
                    tuple(
                        u_ref[res, pl.ds(p * XS + base + at, 8), pl.ds(h * 128, 128)]
                        for p in range(2)
                    )
                    for res in range(XR)
                ]
                for g, (re, im) in enumerate(small_dft(values, -1)):
                    if h == 0:
                        out_ref[g, r, 0, pl.ds(at, 8), :] = re
                        out_ref[g, r, 1, pl.ds(at, 8), :] = im
                    else:
                        out_ref[g, r, 2, pl.ds(at, 8), :] = jnp.where(low_half, re, im)
            return carry
        lax.fori_loop(0, rows // 8, back, 0)


def z_forward_kernel(half_ref, v_ref, high_ref, low_ref, wave_ref, keep_ref, own_ref, other_ref, w_ref):
    lower = half_ref[0] == 0
    rows = v_ref.shape[3]
    low_half = lax.broadcasted_iota(jnp.int32, (rows, 128), 1) < 64

    def group(r, carry):
        real, imag, mixed = ([v_ref[r, j, x] for j in range(4)] for x in range(3))
        p0r, p2r, p0i, p2i, p1r, p1i = [], [], [], [], [], []
        for source, first, second in ((real, p0r, p2r), (imag, p0i, p2i), (mixed, p1r, p1i)):
            for t in range(2):
                a, b = merge(source[2 * t], source[2 * t + 1], low_half)
                first.append(a)
                second.append(b)
        lines = jnp.concatenate(
            [jnp.concatenate(x, axis=1) for x in (p0r + p0i, p1r + p1i, p2r + p2i)], axis=0
        )
        high, low = parts_of(lines)
        w_ref[r] = dot3(high, low, high_ref[r], low_ref[r], ((1,), (1,)))
        return carry
    lax.fori_loop(0, ZR, group, 0)

    def body(i, carry):
        at = pl.multiple_of(i * 8, 8)
        wave_along = wave_ref[pl.ds(at, 8), :]
        keep_along = keep_ref[pl.ds(at, 8), :]
        for lane in range(0, ZS, 128):
            spectra = []
            for j in range(3):
                values = [
                    tuple(
                        w_ref[r, pl.ds(j * rows + at, 8), pl.ds(p * ZS + lane, 128)]
                        for p in range(2)
                    )
                    for r in range(ZR)
                ]
                spectra.append(small_dft(values, -1))
            for place in range(len(LOW)):
                terms = []
                for half, groups in enumerate((LOW, HIGH)):
                    a = groups[place]
                    start = a * ZS + lane - (NZ if half else 0)
                    mode = start + lax.broadcasted_iota(jnp.int32, (8, 128), 1)
                    wave_across = mode.astype(jnp.float32) * (TWO_PI / NZ)
                    keep = jnp.logical_and(3 * jnp.abs(mode) < NZ, keep_along > 0.5)
                    (ar, ai), (br, bi), (cr, ci) = (x[a] for x in spectra)
                    terms.append(
                        [
                            jnp.where(keep, wave_along * ai + wave_across * bi, 0.0),
                            jnp.where(keep, -(wave_along * ar + wave_across * br), 0.0),
                            jnp.where(keep, wave_along * bi + wave_across * ci, 0.0),
                            jnp.where(keep, -(wave_along * br + wave_across * cr), 0.0),
                        ]
                    )
                to = (pl.ds(at, 8), pl.ds(place * ZS + lane, 128))
                for x in range(4):
                    own_ref[(x,) + to] = jnp.where(lower, terms[0][x], terms[1][x])
                    other_ref[(x,) + to] = jnp.where(lower, terms[1][x], terms[0][x])
        return carry
    lax.fori_loop(0, rows // 8, body, 0)


def advance_kernel(half_ref, base_ref, v_ref, old_ref, *refs):
    own_refs, got_refs = refs[:PIECES], refs[PIECES : 2 * PIECES]
    along_ref, across_ref, next_ref, non_ref = refs[2 * PIECES :]
    place = pl.program_id(0)
    is_own = place // PIECES == half_ref[0]
    piece = lax.rem(place, PIECES)
    rows, extent = v_ref.shape[2:]
    wave_along = along_ref[:, :1]
    wave_across = across_ref[:1, :]
    damping = jnp.exp(-VISCOSITY * (wave_along * wave_along + wave_across * wave_across))
    shear = base_ref[0] * wave_along
    empty = jnp.zeros((rows, extent - own_refs[0].shape[2]), jnp.float32)
    for c in range(2):
        for p in range(2):
            term = None
            for h in range(PIECES):
                this = jnp.where(is_own, own_refs[h][2 * c + p], got_refs[h][2 * c + p])
                term = this if term is None else jnp.where(piece == h, this, term)
            term = jnp.where(
                half_ref[0] == 0,
                jnp.concatenate([term, empty], axis=1),
                jnp.concatenate([empty, term], axis=1),
            )
            other = shear * v_ref[c, 1 - p]
            result = term + other if p == 0 else term - other
            non_ref[c, p] = result
            next_ref[c, p] = damping * (
                v_ref[c, p] + TIME_STEP * (GAMMA_NEW * result + ZETA_OLD * old_ref[c, p])
            )


def whole(*_):
    return pl.BlockSpec(memory_space=pltpu.VMEM)


def params(limit):
    return pltpu.CompilerParams(vmem_limit_bytes=limit * MIB)


def kept(block, block_rows):
    start = block * block_rows
    return jnp.logical_or(3 * start < NX, 3 * (NX - start - block_rows + 1) < NX)


def exchange_kernel(block_rows, src_ref, dst_ref, send_sems, recv_sems, own_sem):
    across = lax.axis_size("gz")
    count = lax.axis_size("gx") * across
    me = lax.axis_index("gx") * across + lax.axis_index("gz")

    def device(t):
        return (t // across, lax.rem(t, across))

    def wanted(t):
        return kept(t, block_rows) if block_rows else t >= 0

    barrier = pltpu.get_barrier_semaphore()

    def greet(i, carry):
        pl.semaphore_signal(
            barrier,
            inc=1,
            device_id=device(lax.rem(me + i, count)),
            device_id_type=pl.DeviceIdType.MESH,
        )
        return carry

    lax.fori_loop(1, count, greet, 0)
    pl.semaphore_wait(barrier, count - 1)

    def copy(i):
        t = lax.rem(me + i, count)
        return pltpu.make_async_remote_copy(
            src_ref=src_ref.at[t],
            dst_ref=dst_ref.at[me],
            send_sem=send_sems.at[i],
            recv_sem=recv_sems.at[i],
            device_id=device(t),
            device_id_type=pl.DeviceIdType.MESH,
        )

    def start(i, carry):
        @pl.when(wanted(lax.rem(me + i, count)))
        def _():
            copy(i).start()

        return carry

    lax.fori_loop(1, count, start, 0)
    own = pltpu.make_async_copy(src_ref.at[me], dst_ref.at[me], own_sem)
    own.start()
    own.wait()

    def finish(i, carry):
        @pl.when(wanted(lax.rem(me + i, count)))
        def _():
            copy(i).wait_send()

        @pl.when(wanted(me))
        def _():
            copy(i).wait_recv()

        return carry

    lax.fori_loop(1, count, finish, 0)


def exchange(value, number, block_rows=0):
    count = value.shape[0]
    return pl.pallas_call(
        functools.partial(exchange_kernel, block_rows),
        out_shape=jax.ShapeDtypeStruct(value.shape, value.dtype),
        in_specs=[pl.BlockSpec(memory_space=pl.ANY)],
        out_specs=pl.BlockSpec(memory_space=pl.ANY),
        scratch_shapes=[
            pltpu.SemaphoreType.DMA((count,)),
            pltpu.SemaphoreType.DMA((count,)),
            pltpu.SemaphoreType.DMA,
        ],
        compiler_params=pltpu.CompilerParams(collective_id=number, has_side_effects=True),
        cost_estimate=pl.CostEstimate(flops=0, bytes_accessed=64 * value.size, transcendentals=0),
        name="exchange_" + str(number),
    )(value)


def lines_local(velocity, previous, base_flow):
    velocity, previous = velocity[:, :, 0], previous[:, :, 0]
    mode_count, extent = velocity.shape[2:]
    rows = mode_count // 2
    gx, gz = lax.axis_index("gx"), lax.axis_index("gz")
    f32, bf16 = jnp.float32, jnp.bfloat16
    zh, zl = z_table()
    xh, xl = x_table()
    fh, fl = np.swapaxes(xh, 1, 2), np.swapaxes(xl, 1, 2)

    piece = rows // PIECES
    half = gz.astype(jnp.int32)[None]
    scalar = pl.BlockSpec(memory_space=pltpu.SMEM)
    swap = [(0, 1), (1, 0)]
    got, swapped = [], []
    for h in range(PIECES):
        part = lax.dynamic_slice_in_dim(velocity, (1 - gz) * rows + h * piece, piece, axis=2)
        if h:
            part, got[h - 1] = lax.optimization_barrier((part, got[h - 1]))
        got.append(lax.ppermute(part, "gz", swap))
    for h in range(PIECES):
        mine = lax.dynamic_slice_in_dim(velocity, gz * rows + h * piece, piece, axis=2)
        if h:
            mine, swapped[h - 1] = lax.optimization_barrier((mine, swapped[h - 1]))
        along_z = pl.pallas_call(
            z_inverse_kernel,
            out_shape=jax.ShapeDtypeStruct((ZR, 4, 2, piece, 128), f32),
            in_specs=[scalar] + [whole()] * 4,
            out_specs=whole(),
            scratch_shapes=[pltpu.VMEM((ZR, 2 * piece, 2 * ZS), bf16)] * 2,
            compiler_params=params(40),
            name="z_inverse",
        )(half, mine, got[h], zh, zl)
        swapped.append(exchange(along_z.reshape(32, 2, piece, 128), 1 + h))
    worked = pl.pallas_call(
        x_kernel,
        out_shape=[jax.ShapeDtypeStruct((XR, 2, 3, piece, 128), f32)] * PIECES,
        in_specs=[whole()] * (PIECES + 4),
        out_specs=[whole()] * PIECES,
        scratch_shapes=[pltpu.VMEM((XR, 2 * XS, 128), bf16)] * 2
        + [pltpu.VMEM((XR, 2 * XS, 256), f32)],
        compiler_params=params(56),
        name="x_work",
    )(*(x.reshape(XR, 2, 2, piece, 128) for x in swapped), xh, xl, fh, fl)

    def modes(start, count, size):
        numbers = start + jnp.arange(count, dtype=jnp.int32)
        return jnp.where(2 * numbers < size, numbers, numbers - size)

    own = modes(gx * mode_count + gz * rows, rows, NX)[:, None]
    own_wave = jnp.broadcast_to(own.astype(f32) * (TWO_PI / NX), (rows, 128))
    own_keep = jnp.broadcast_to((3 * jnp.abs(own) < NX).astype(f32), (rows, 128))
    active = len(LOW) * ZS
    own_terms, got_terms = [], []
    for h in range(PIECES):
        sent = worked[h].reshape(32, 3, piece, 128)
        if h:
            sent, own_terms[h - 1] = lax.optimization_barrier((sent, own_terms[h - 1]))
        returned = exchange(sent, 1 + PIECES + h, rows)
        at = slice(h * piece, (h + 1) * piece)
        mine, other = pl.pallas_call(
            z_forward_kernel,
            out_shape=[jax.ShapeDtypeStruct((4, piece, active), f32)] * 2,
            in_specs=[scalar] + [whole()] * 5,
            out_specs=[whole()] * 2,
            scratch_shapes=[pltpu.VMEM((ZR, 3 * piece, 2 * ZS), f32)],
            compiler_params=params(40),
            name="z_forward",
        )(half, returned.reshape(ZR, 4, 3, piece, 128), zh, zl, own_wave[at], own_keep[at])
        own_terms.append(mine)
        got_terms.append(lax.ppermute(other, "gz", swap))

    along = modes(gx * mode_count, mode_count, NX).astype(f32) * (TWO_PI / NX)
    across = modes(gz * extent, extent, NZ).astype(f32) * (TWO_PI / NZ)
    block = piece
    field = pl.BlockSpec((2, 2, block, extent), lambda i: (0, 0, i, 0))
    advanced, nonlinear = pl.pallas_call(
        advance_kernel,
        grid=(mode_count // block,),
        out_shape=[jax.ShapeDtypeStruct(velocity.shape, f32)] * 2,
        in_specs=[
            scalar,
            scalar,
            field,
            field,
            *([pl.BlockSpec((4, block, active), lambda i: (0, 0, 0))] * (2 * PIECES)),
            pl.BlockSpec((block, 128), lambda i: (i, 0)),
            pl.BlockSpec((8, extent), lambda i: (0, 0)),
        ],
        out_specs=[field, field],
        compiler_params=params(48),
        name="advance",
    )(
        half,
        base_flow,
        velocity,
        previous,
        *own_terms,
        *got_terms,
        jnp.broadcast_to(along[:, None], (mode_count, 128)),
        jnp.broadcast_to(across[None], (8, extent)),
    )
    return advanced[:, :, None], nonlinear[:, :, None]


def solution(mesh):
    in_specs = (P(None, None, None, "gx", "gz"), P(None, None, None, "gx", "gz"), P())
    out_specs = (P(None, None, None, "gx", "gz"), P(None, None, None, "gx", "gz"))
    fits = mesh.shape["gx"] == XR and mesh.shape["gz"] == 2
    work = lines_local if fits else local
    return jax.shard_map(work, mesh=mesh, in_specs=in_specs, out_specs=out_specs, check_vma=False)
```
